256 devices in a mesh: row: 16 (over z, y_hi), col: 16 (over y_lo, x, core).
Axes of the slice: x: 4, y: 4 (y_hi: 2, y_lo: 2; y = y_hi * 2 + y_lo), z: 8, core: 2. Of those that a mesh axis runs over, the one named last changes fastest.
Arguments:
- acts_panel: bfloat16 [8192, 1024], P('row', 'col')
- acts_trail: bfloat16 [8192, 32768], P('row', 'col')
- weight_panel: float32 [16384, 1024], P('row', 'col'), may hold values from -6 to 6
- block_order: int32 [8], replicated, may hold values from 0 to 7, each once
Outputs:
- slab_factor: float32 [1024, 32768], P('row', 'col')
- pruned_weight: float32 [16384, 1024], P('row', 'col')
The draws below stay inside these ranges and needn't reach their ends.
Inputs may be any that keep to these rules, and one draw needn't show every extreme that they name: `block_order`: each block number once.
All inputs are finite; a program needn't handle non-finite values.
Results may differ from the reference program's by a relative error of at most 0.0003.
Values may be sent and summed in bfloat16 or wider, within the bound.
No kernel may reach another device: no remote copies, remote signals or barrier semaphores. Data moves between devices by JAX's collectives and lax.ppermute only.
A program may use at most 128 MiB of HBM per device.

```python
import math
import jax
import jax.numpy as jnp
from jax import lax

OUT = 16384
PANEL = 1024
TRAIL = 32768
NB = 128
NPRUNE = 4
NBLK = 8
TOKENS = 8192


def panel_values(key):
    keys = jax.random.split(key, 6)
    base = jax.random.normal(keys[0], (TOKENS, PANEL), jnp.float32)
    first = jax.random.permutation(keys[1], PANEL)
    second = jax.random.permutation(keys[2], PANEL)
    gains = jax.random.uniform(keys[3], (2, PANEL), jnp.float32, -0.8, 0.8)
    scales = jnp.exp(jax.random.uniform(keys[4], (PANEL,), jnp.float32, math.log(0.4), math.log(4.0)))
    token_scale = jnp.exp(jax.random.uniform(keys[5], (TOKENS, 1), jnp.float32, math.log(0.5), math.log(2.0)))
    mixed = base + gains[0] * base[:, first] + gains[1] * base[:, second]
    return mixed * scales * token_scale


def draw_acts_panel(key, part):
    values = panel_values(key)
    return jnp.clip(values, -24.0, 24.0).astype(jnp.bfloat16)


def draw_acts_trail(key, part):
    panel = panel_values(key)
    key = jax.random.fold_in(key, 23)
    keys = jax.random.split(key, 3)
    mixing = jax.random.uniform(keys[0], (TRAIL,), jnp.float32, -1.2, 1.2)
    noise_scale = jnp.exp(jax.random.uniform(keys[1], (TRAIL,), jnp.float32, math.log(0.3), math.log(3.0)))
    noise = jax.random.normal(keys[2], (TOKENS, TRAIL), jnp.float32) * noise_scale
    partner = jnp.tile(panel, (1, TRAIL // PANEL))
    values = mixing * partner + noise
    return jnp.clip(values, -24.0, 24.0).astype(jnp.bfloat16)


def shard_levels(stream_key, dims, cuts, low, top_value):
    def one(dim, shards_of):
        steps = jax.random.uniform(jax.random.fold_in(jax.random.fold_in(stream_key, 6), dim), (shards_of,), jnp.float32, low / len(cuts), top_value / len(cuts))
        return jnp.repeat(jnp.exp(steps), dims[dim] // shards_of).reshape((-1,) + (1,) * (len(dims) - dim - 1))

    loudness = one(*cuts[0])
    for cut in cuts[1:]:
        loudness = loudness * one(*cut)
    return loudness


def scatter_about(key, extent, spread, limit, pieces=(), held_as=jnp.bfloat16):
    factor_of = shard_levels(key, extent, pieces, -0.22, 0.18) if pieces else 1.0
    values = jax.random.normal(key, extent, jnp.float32) * spread * factor_of
    return jnp.minimum(jnp.maximum(values, -limit), limit).astype(held_as)


def setup_inputs(seed: int = 0) -> dict:
    key_list = jax.random.split(jax.random.key(seed), 5)
    return {
        "acts_panel": draw_acts_panel(jax.random.fold_in(key_list[4], 71), 0),
        "acts_trail": draw_acts_trail(jax.random.fold_in(key_list[4], 71), 0),
        "weight_panel": scatter_about(key_list[2], (OUT, PANEL), 1.0, 6.0, ((0, 16), (1, 16)), jnp.float32),
        "block_order": jax.random.permutation(key_list[3], NBLK).astype(jnp.int32),
    }


DAMP_SHARE = 0.01

def choose(block_order):
    offsets = jnp.arange(NB, dtype=jnp.int32)
    chosen = (block_order[:NPRUNE, None].astype(jnp.int32) * NB + offsets[None, :]).reshape(-1)
    channels = jnp.arange(PANEL, dtype=jnp.int32)
    return (channels[:, None] == chosen[None, :]).astype(jnp.float32)

def factorize(gram_panel):
    mean_diag = jnp.mean(jnp.diagonal(gram_panel))
    identity = jnp.eye(PANEL, dtype=jnp.float32)
    hessian = gram_panel + DAMP_SHARE * mean_diag * identity
    factor = jnp.linalg.cholesky(hessian)
    return lax.linalg.triangular_solve(factor, identity, left_side=True, lower=True)

def reference(acts_panel, acts_trail, weight_panel, block_order):
    high = lax.Precision.HIGHEST
    gram_panel = jnp.dot(acts_panel.T.astype(jnp.float32), acts_panel.astype(jnp.float32), preferred_element_type=jnp.float32) / TOKENS
    inverse_factor = factorize(gram_panel)
    slab = jnp.dot(acts_panel.T.astype(jnp.float32), acts_trail.astype(jnp.float32), preferred_element_type=jnp.float32) / TOKENS
    slab_factor = jnp.dot(inverse_factor, slab, precision=high)
    select = choose(block_order)
    inverse_cols = jnp.dot(inverse_factor, select, precision=high)
    inverse_block = jnp.dot(inverse_cols.T, inverse_cols, precision=high)
    inverse_rows = jnp.dot(inverse_cols.T, inverse_factor, precision=high)
    pruned_cols = jnp.dot(weight_panel, select, precision=high)
    block_root = jnp.linalg.cholesky(inverse_block)
    middle = lax.linalg.triangular_solve(block_root, pruned_cols.T, left_side=True, lower=True)
    coefficients = lax.linalg.triangular_solve(block_root, middle, left_side=True, lower=True, transpose_a=True)
    pruned_weight = weight_panel - jnp.dot(coefficients.T, inverse_rows, precision=high)
    return (slab_factor, pruned_weight)
```

```python
import functools

import jax
import jax.numpy as jnp
from jax import lax
from jax.experimental import pallas as pl
from jax.experimental.pallas import tpu as pltpu
from jax.sharding import PartitionSpec as P

f32 = jnp.float32
NB = 128
HIGH = lax.Precision.HIGHEST

def lanes(x):
    return jnp.broadcast_to(x, (8, NB))

def factor_blocks(blocks):
    lane = lax.broadcasted_iota(jnp.int32, (8, NB), 1)
    sub = lax.broadcasted_iota(jnp.int32, (8, NB), 0)
    at = [sub == k for k in range(8)]
    outs = [[] for _ in blocks]
    for j in range(16):
        lo = 8 * j
        inside = (lane >= lo) & (lane < lo + 8)
        unit = jnp.where(lane - lo == sub, 1.0, 0.0).astype(f32)
        for b, rows in enumerate(blocks):
            R = rows[j]
            D = [lanes(R[:, lo + k:lo + k + 1]) for k in range(8)]
            R = jnp.where(inside, unit, R)
            out = jnp.zeros((8, NB), f32)
            for k in range(8):
                p = lanes(D[k][k:k + 1, :])
                inv = 1.0 / p
                bR = lanes(R[k:k + 1, :])
                out = jnp.where(at[k], bR * lax.rsqrt(p), out)
                f = D[k] * inv
                R = jnp.where(at[k], bR * inv, R - f * bR)
                for m in range(k + 1, 8):
                    bD = lanes(D[m][k:k + 1, :])
                    D[m] = jnp.where(at[k], bD * inv, D[m] - f * bD)
            outs[b].append(jnp.where(lane <= lo + sub, out, 0.0))
            if j < 15:
                W = [lanes(R[k:k + 1, :]) for k in range(8)]
                for i in range(j + 1, 16):
                    T = rows[i]
                    acc = lanes(T[:, lo:lo + 1]) * W[0]
                    for k in range(1, 8):
                        acc += lanes(T[:, lo + k:lo + k + 1]) * W[k]
                    rows[i] = jnp.where(inside, 0.0, T) - acc
    return outs

def load_block(ref, k):
    o = pl.multiple_of(k * NB, NB)
    return [ref[pl.ds(pl.multiple_of(o + 8 * i, 8), 8), pl.ds(o, NB)] for i in range(16)]

def eliminate(ref, inv_ref, k, n):
    o = pl.multiple_of(k * NB, NB)
    eye = jnp.where(lax.broadcasted_iota(jnp.int32, (NB, NB), 0) == lax.broadcasted_iota(jnp.int32, (NB, NB), 1), 1.0, 0.0).astype(f32)
    ref[pl.ds(o, NB), pl.ds(o, NB)] = eye
    U = jnp.dot(inv_ref[...], ref[pl.ds(o, NB), :], precision=HIGH, preferred_element_type=f32)
    ref[pl.ds(o, NB), :] = U

    def below(i, _):
        w = pl.multiple_of(i * NB, NB)
        Ui = ref[pl.ds(o, NB), pl.ds(w, NB)]
        ref[pl.ds(w, NB), pl.ds(o, NB)] = jnp.zeros((NB, NB), f32)
        ref[pl.ds(w, NB), :] -= lax.dot_general(Ui, ref[pl.ds(o, NB), :], (((0,), (0,)), ((), ())), precision=HIGH, preferred_element_type=f32)
        return 0
    lax.fori_loop(k + 1, n, below, 0)

def kernel(tokens, order_ref, own_ref, g_ref, x_ref, m_ref, at, inv1, inv2, hst):
    r = lax.broadcasted_iota(jnp.int32, (NB, NB), 0)
    c = lax.broadcasted_iota(jnp.int32, (NB, NB), 1)
    diag = r == c
    tot = jnp.zeros((NB, NB), f32)
    for b in range(8):
        tot += jnp.where(diag, g_ref[b * NB:(b + 1) * NB, b * NB:(b + 1) * NB], 0.0)
    damp = jnp.sum(tot) * (0.01 / 1024.0 / tokens)
    x_ref[...] = g_ref[...] * (1.0 / tokens)
    for b in range(8):
        s = slice(b * NB, (b + 1) * NB)
        x_ref[s, s] += jnp.where(diag, damp, 0.0)
    for a in range(4):
        oa = pl.multiple_of(order_ref[4 + a] * NB, NB)
        os = pl.multiple_of(order_ref[a] * NB, NB)
        for b in range(4):
            ob = pl.multiple_of(order_ref[4 + b] * NB, NB)
            at[a * NB:(a + 1) * NB, b * NB:(b + 1) * NB] = x_ref[pl.ds(oa, NB), pl.ds(ob, NB)]
            hst[a * NB:(a + 1) * NB, b * NB:(b + 1) * NB] = x_ref[pl.ds(os, NB), pl.ds(ob, NB)]

    def both(k, _):
        o1, o2 = factor_blocks([load_block(x_ref, k), load_block(at, k)])
        for i in range(16):
            inv1[8 * i:8 * i + 8, :] = o1[i]
            inv2[8 * i:8 * i + 8, :] = o2[i]
        eliminate(x_ref, inv1, k, 8)
        eliminate(at, inv2, k, 4)
        return 0
    lax.fori_loop(0, 4, both, 0)

    def single(k, _):
        o1, = factor_blocks([load_block(x_ref, k)])
        for i in range(16):
            inv1[8 * i:8 * i + 8, :] = o1[i]
        eliminate(x_ref, inv1, k, 8)
        return 0
    lax.fori_loop(4, 8, single, 0)
    for k in range(7):
        x_ref[k * NB:(k + 1) * NB, (k + 1) * NB:] = jnp.zeros((NB, (7 - k) * NB), f32)
    for k in range(3):
        at[k * NB:(k + 1) * NB, (k + 1) * NB:] = jnp.zeros((NB, (3 - k) * NB), f32)
    own = own_ref[0]
    m_ref[...] = jnp.zeros((512, NB), f32)
    for a in range(4):
        @pl.when(order_ref[a] == own)
        def _():
            m_ref[a * NB:(a + 1) * NB, :] = jnp.where(diag, 1.0, 0.0)
        @pl.when(order_ref[4 + a] == own)
        def _():
            z = lax.dot_general(at[...], at[:, a * NB:(a + 1) * NB], (((0,), (0,)), ((), ())), precision=HIGH, preferred_element_type=f32)
            m_ref[...] = -jnp.dot(hst[...], z, precision=HIGH, preferred_element_type=f32)

def factor_call(gram, order, own, tokens):
    return pl.pallas_call(
        functools.partial(kernel, tokens),
        out_shape=(jax.ShapeDtypeStruct((1024, 1024), f32), jax.ShapeDtypeStruct((512, NB), f32)),
        in_specs=[pl.BlockSpec(memory_space=pltpu.SMEM), pl.BlockSpec(memory_space=pltpu.SMEM), pl.BlockSpec(memory_space=pltpu.VMEM)],
        out_specs=(pl.BlockSpec(memory_space=pltpu.VMEM), pl.BlockSpec(memory_space=pltpu.VMEM)),
        scratch_shapes=[pltpu.VMEM((512, 512), f32), pltpu.VMEM((NB, NB), f32), pltpu.VMEM((NB, NB), f32), pltpu.VMEM((512, 512), f32)],
        compiler_params=pltpu.CompilerParams(vmem_limit_bytes=40 * 1024 * 1024),
    )(order, own, gram)


def slab_kernel(panel_ref, trail_ref, out_ref):
    @pl.when(pl.program_id(0) == 0)
    def _():
        out_ref[...] = jnp.zeros_like(out_ref)

    out_ref[...] += jnp.dot(panel_ref[0], trail_ref[0], preferred_element_type=f32)


def slab_call(panel, trail):
    groups, channels, span = panel.shape
    columns = trail.shape[2]
    return pl.pallas_call(
        slab_kernel,
        grid=(groups,),
        in_specs=[
            pl.BlockSpec((1, channels, span), lambda i: (i, 0, 0)),
            pl.BlockSpec((1, span, columns), lambda i: (i, 0, 0)),
        ],
        out_specs=pl.BlockSpec((channels, columns), lambda i: (0, 0)),
        out_shape=jax.ShapeDtypeStruct((channels, columns), f32),
    )(panel, trail)


def spread(x, axis):
    n = lax.axis_size(axis)
    return lax.all_to_all(jnp.broadcast_to(x[None], (n,) + x.shape), axis, 0, 0)


def on_device(acts_panel, acts_trail, weight_panel, block_order):
    n_row = lax.axis_size("row")
    span, own_n = acts_panel.shape
    tokens = span * n_row
    own_t = acts_panel.T
    everything = lax.all_gather(own_t, ("row", "col"))
    panel_t = spread(own_t, "col").reshape(-1, span)
    strip = lax.dot_general(own_t, panel_t, (((1,), (1,)), ((), ())), preferred_element_type=f32)
    pieces = strip.reshape(8, 8, 2, 512).transpose(0, 2, 1, 3).reshape(16, 8, 512)
    piece = lax.all_to_all(pieces, "row", 0, 0).sum(0)
    strip_total = spread(piece, "row").reshape(8, 2, 8, 512).transpose(0, 2, 1, 3).reshape(64, 1024)
    trail_in, strip_total = lax.optimization_barrier((acts_trail, strip_total))
    gram = spread(strip_total, "col").reshape(1024, 1024)
    trail = lax.all_to_all(trail_in.reshape(span, n_row, -1), "row", 1, 0)
    weight_t = weight_panel.T
    weight_in, gram = lax.optimization_barrier((weight_t, gram))
    weight_all = spread(weight_in, "col").reshape(1024, -1)
    own = lax.axis_index("col")
    inverse_factor, mixing = factor_call(gram, block_order, (own // 2).reshape(1), tokens)
    everything, inverse_factor = lax.optimization_barrier((everything, inverse_factor))
    slab = slab_call(everything.reshape(n_row, 1024, span), trail) * (1.0 / tokens)
    solved = jnp.dot(inverse_factor, slab, precision=HIGH)
    slab_rows = lax.all_to_all(solved.reshape(n_row, 1024 // n_row, -1), "row", 0, 0)
    slab_factor = slab_rows.transpose(1, 0, 2).reshape(1024 // n_row, -1)
    pruned = jnp.concatenate(
        [lax.dynamic_slice_in_dim(weight_all, block_order[q] * NB, NB, 0) for q in range(4)], 0
    )
    own_mixing = lax.dynamic_slice_in_dim(mixing, (own % 2) * own_n, own_n, 1)
    change = lax.dot_general(own_mixing, pruned, (((0,), (0,)), ((), ())), precision=HIGH)
    return (slab_factor, (weight_t - change).T)


def solution(mesh):
    return jax.shard_map(
        on_device,
        mesh=mesh,
        in_specs=(P("row", "col"), P("row", "col"), P("row", "col"), P()),
        out_specs=(P("row", "col"), P("row", "col")),
        check_vma=False,
    )
```

```python
import functools

import jax
import jax.numpy as jnp
from jax import lax
from jax.experimental import pallas as pl
from jax.experimental.pallas import tpu as pltpu
from jax.sharding import PartitionSpec as P

f32 = jnp.float32
NB = 128
HIGH = lax.Precision.HIGHEST

def lanes(x):
    return jnp.broadcast_to(x, (8, NB))

def factor_blocks(blocks):
    lane = lax.broadcasted_iota(jnp.int32, (8, NB), 1)
    sub = lax.broadcasted_iota(jnp.int32, (8, NB), 0)
    at = [sub == k for k in range(8)]
    outs = [[] for _ in blocks]
    for j in range(16):
        lo = 8 * j
        inside = (lane >= lo) & (lane < lo + 8)
        unit = jnp.where(lane - lo == sub, 1.0, 0.0).astype(f32)
        for b, rows in enumerate(blocks):
            R = rows[j]
            D = [lanes(R[:, lo + k:lo + k + 1]) for k in range(8)]
            E = {(a, m): lanes(D[m][a:a + 1, :]) for m in range(8) for a in range(m, 8)}
            R = jnp.where(inside, unit, R)
            t = [lanes(R[k:k + 1, :]) for k in range(8)]
            inv, low = [], {}
            out = jnp.zeros((8, NB), f32)
            for k in range(8):
                p = E[k, k]
                inv.append(pl.reciprocal(p, approx=False))
                out = jnp.where(at[k], t[k] * lax.rsqrt(p), out)
                for a in range(k + 1, 8):
                    low[a, k] = E[a, k] * inv[k]
                    t[a] = t[a] - low[a, k] * t[k]
                    for m in range(k + 1, a + 1):
                        E[a, m] = E[a, m] - low[a, k] * E[m, k]
            outs[b].append(jnp.where(lane <= lo + sub, out, 0.0))
            if j < 15:
                w = [t[k] * inv[k] for k in range(8)]
                for k in range(7, 0, -1):
                    for a in range(k):
                        w[a] = w[a] - low[k, a] * w[k]
                for i in range(j + 1, 16):
                    T = rows[i]
                    terms = [lanes(T[:, lo + k:lo + k + 1]) * w[k] for k in range(7, -1, -1)]
                    T = jnp.where(inside, 0.0, T)
                    for x in terms:
                        T = T - x
                    rows[i] = T
    return outs

def load_block(ref, k):
    o = pl.multiple_of(k * NB, NB)
    return [ref[pl.ds(pl.multiple_of(o + 8 * i, 8), 8), pl.ds(o, NB)] for i in range(16)]

def split3(x):
    a = x.astype(jnp.bfloat16)
    r = x - a.astype(f32)
    b = r.astype(jnp.bfloat16)
    return a, b, (r - b.astype(f32)).astype(jnp.bfloat16)

def stack_left(x):
    a, b, c = split3(x)
    return jnp.concatenate([a, a, b, b, a, c], 1)

def stack_right(x):
    a, b, c = split3(x)
    return jnp.concatenate([a, b, a, b, c, a], 0)

def prepare(ref, inv_ref, right, k, n):
    o = pl.multiple_of(k * NB, NB)
    eye = jnp.where(lax.broadcasted_iota(jnp.int32, (NB, NB), 0) == lax.broadcasted_iota(jnp.int32, (NB, NB), 1), 1.0, 0.0).astype(f32)
    ref[pl.ds(o, NB), pl.ds(o, NB)] = eye
    left = stack_left(inv_ref[...])
    for h in range(n // 4):
        s = slice(h * 512, h * 512 + 512)
        U = jnp.dot(left, stack_right(ref[pl.ds(o, NB), s]), preferred_element_type=f32)
        ref[pl.ds(o, NB), s] = U
        right[:, s] = stack_right(U)

def eliminate(ref, right, k, n):
    for c in range(n - 1):
        @pl.when(k == c)
        def _():
            o, d = c * NB, (c + 1) * NB
            left = stack_left(ref[o:d, d:n * NB].T)
            ref[d:n * NB, o:d] = jnp.zeros((n * NB - d, NB), f32)
            if (n - 1 - c) < 4:
                ref[d:n * NB, :] -= jnp.dot(left, right[:, :n * NB], preferred_element_type=f32)
            else:
                m = (c + 1 + n) // 2 * NB
                ref[d:m, :] -= jnp.dot(left[:m - d], right[:, :n * NB], preferred_element_type=f32)
                ref[m:n * NB, :d] -= jnp.dot(left[m - d:], right[:, :d], preferred_element_type=f32)
                ref[m:n * NB, m:] -= jnp.dot(left[m - d:], right[:, m:n * NB], preferred_element_type=f32)

def kernel(tokens, order_ref, own_ref, g_ref, x_ref, m_ref, at, inv1, inv2, hst, right):
    r = lax.broadcasted_iota(jnp.int32, (NB, NB), 0)
    c = lax.broadcasted_iota(jnp.int32, (NB, NB), 1)
    diag = r == c
    tot = jnp.zeros((NB, NB), f32)
    for b in range(8):
        tot += jnp.where(diag, g_ref[b * NB:(b + 1) * NB, :NB], 0.0)
    scale = 1.0 / tokens
    damp = jnp.sum(tot) * (0.01 / 1024.0 / tokens)
    for a in range(8):
        for b in range(a, 8):
            if b - a <= 4:
                v = g_ref[a * NB:(a + 1) * NB, (b - a) * NB:(b - a + 1) * NB]
            else:
                v = g_ref[b * NB:(b + 1) * NB, (8 + a - b) * NB:(9 + a - b) * NB].T
            v = v * scale
            if a == b:
                v = v + jnp.where(diag, damp, 0.0)
            x_ref[a * NB:(a + 1) * NB, b * NB:(b + 1) * NB] = v
    for a in range(4):
        ta, sa = order_ref[4 + a], order_ref[a]
        oa = pl.multiple_of(ta * NB, NB)
        os = pl.multiple_of(sa * NB, NB)
        for b in range(4):
            tb = order_ref[4 + b]
            ob = pl.multiple_of(tb * NB, NB)
            if a <= b:
                at[a * NB:(a + 1) * NB, b * NB:(b + 1) * NB] = x_ref[pl.ds(oa, NB), pl.ds(ob, NB)]

            @pl.when(sa < tb)
            def _():
                hst[a * NB:(a + 1) * NB, b * NB:(b + 1) * NB] = x_ref[pl.ds(os, NB), pl.ds(ob, NB)]

            @pl.when(sa > tb)
            def _():
                hst[a * NB:(a + 1) * NB, b * NB:(b + 1) * NB] = x_ref[pl.ds(ob, NB), pl.ds(os, NB)].T

    def both(k, _):
        o1, o2 = factor_blocks([load_block(x_ref, k), load_block(at, k)])
        for i in range(16):
            inv1[8 * i:8 * i + 8, :] = o1[i]
            inv2[8 * i:8 * i + 8, :] = o2[i]
        prepare(x_ref, inv1, right, k, 8)
        eliminate(x_ref, right, k, 8)
        prepare(at, inv2, right, k, 4)
        eliminate(at, right, k, 4)
        return 0
    lax.fori_loop(0, 4, both, 0)

    def single(k, _):
        o1, = factor_blocks([load_block(x_ref, k)])
        for i in range(16):
            inv1[8 * i:8 * i + 8, :] = o1[i]
        prepare(x_ref, inv1, right, k, 8)
        eliminate(x_ref, right, k, 8)
        return 0
    lax.fori_loop(4, 8, single, 0)
    for k in range(7):
        x_ref[k * NB:(k + 1) * NB, (k + 1) * NB:] = jnp.zeros((NB, (7 - k) * NB), f32)
    for k in range(3):
        at[k * NB:(k + 1) * NB, (k + 1) * NB:] = jnp.zeros((NB, (3 - k) * NB), f32)
    own = own_ref[0]
    for a in range(4):
        @pl.when(order_ref[a] == own)
        def _():
            m_ref[...] = jnp.zeros((512, NB), f32)
            m_ref[a * NB:(a + 1) * NB, :] = jnp.where(diag, 1.0, 0.0)
        @pl.when(order_ref[4 + a] == own)
        def _():
            z = lax.dot_general(at[...], at[:, a * NB:(a + 1) * NB], (((0,), (0,)), ((), ())), precision=HIGH, preferred_element_type=f32)
            m_ref[...] = -jnp.dot(hst[...], z, precision=HIGH, preferred_element_type=f32)

def factor_call(gram, order, own, tokens):
    return pl.pallas_call(
        functools.partial(kernel, tokens),
        out_shape=(jax.ShapeDtypeStruct((1024, 1024), f32), jax.ShapeDtypeStruct((512, NB), f32)),
        in_specs=[pl.BlockSpec(memory_space=pltpu.SMEM), pl.BlockSpec(memory_space=pltpu.SMEM), pl.BlockSpec(memory_space=pltpu.VMEM)],
        out_specs=(pl.BlockSpec(memory_space=pltpu.VMEM), pl.BlockSpec(memory_space=pltpu.VMEM)),
        scratch_shapes=[pltpu.VMEM((512, 512), f32), pltpu.VMEM((NB, NB), f32), pltpu.VMEM((NB, NB), f32), pltpu.VMEM((512, 512), f32), pltpu.VMEM((768, 1024), jnp.bfloat16)],
        compiler_params=pltpu.CompilerParams(vmem_limit_bytes=40 * 1024 * 1024),
    )(order, own, gram)


def slab_kernel(tokens, panel_ref, trail_ref, inverse_ref, out_ref, total):
    @pl.when(pl.program_id(0) == 0)
    def _():
        total[...] = jnp.zeros_like(total)

    for g in range(panel_ref.shape[0]):
        total[...] += jnp.dot(panel_ref[g], trail_ref[g], preferred_element_type=f32)

    @pl.when(pl.program_id(0) == pl.num_programs(0) - 1)
    def _():
        slab = total[...] * (1.0 / tokens)
        for h in range(4):
            s = slice(256 * h, 256 * h + 256)
            e = 256 * h + 256
            out_ref[s, :] = jnp.dot(inverse_ref[s, :e], slab[:e], precision=HIGH, preferred_element_type=f32)


def slab_call(panel, trail, inverse, tokens):
    groups, channels, span = panel.shape
    columns = trail.shape[2]
    each = 2
    return pl.pallas_call(
        functools.partial(slab_kernel, tokens),
        grid=(groups // each,),
        in_specs=[
            pl.BlockSpec((each, channels, span), lambda i: (i, 0, 0)),
            pl.BlockSpec((each, span, columns), lambda i: (i, 0, 0)),
            pl.BlockSpec((channels, channels), lambda i: (0, 0)),
        ],
        out_specs=pl.BlockSpec((channels, columns), lambda i: (0, 0)),
        out_shape=jax.ShapeDtypeStruct((channels, columns), f32),
        scratch_shapes=[pltpu.VMEM((channels, columns), f32)],
        compiler_params=pltpu.CompilerParams(vmem_limit_bytes=40 * 1024 * 1024),
    )(panel, trail, inverse)


def spread(x, axis):
    n = lax.axis_size(axis)
    return lax.all_to_all(jnp.broadcast_to(x[None], (n,) + x.shape), axis, 0, 0)


def ascending(blocks):
    place = jnp.sum((blocks[None, :] < blocks[:, None]).astype(jnp.int32), 1)
    slot = jnp.arange(blocks.shape[0], dtype=jnp.int32)
    return jnp.sum(jnp.where(place[None, :] == slot[:, None], blocks[None, :], 0), 1)


def on_device(acts_panel, acts_trail, weight_panel, block_order):
    n_row = lax.axis_size("row")
    span, own_n = acts_panel.shape
    tokens = span * n_row
    own = lax.axis_index("col")
    own_t = acts_panel.T
    everything = lax.all_gather(own_t, ("row", "col"))
    panel_t = spread(own_t, "col").reshape(-1, span)
    strip = lax.dot_general(own_t, panel_t, (((1,), (1,)), ((), ())), preferred_element_type=f32)
    pieces = strip.reshape(8, 8, 2, 512).transpose(0, 2, 1, 3).reshape(16, 8, 512)
    piece = lax.all_to_all(pieces, "row", 0, 0).sum(0)
    strip_total = spread(piece, "row").reshape(8, 2, 8, 512).transpose(0, 2, 1, 3).reshape(64, 1024)
    twice = jnp.concatenate([strip_total, strip_total[:, :512]], 1)
    band = lax.dynamic_slice_in_dim(twice, own // 2 * NB, 5 * NB, 1)
    gram = spread(band, "col").reshape(1024, 5 * NB)
    weight_t = weight_panel.T
    columns = acts_trail.shape[1] // n_row
    trail_cut = acts_trail.reshape(span, n_row, columns).transpose(1, 0, 2)
    weight_in, trail_cut, gram = lax.optimization_barrier((weight_t, trail_cut, gram))
    trail = lax.all_to_all(trail_cut, "row", 0, 0)
    weight_all = lax.all_gather(weight_in, "col", axis=0, tiled=True)
    order = jnp.concatenate([block_order[:4], ascending(block_order[4:])])
    inverse_factor, mixing = factor_call(gram, order, (own // 2).reshape(1), tokens)
    everything, trail, mixing = lax.optimization_barrier((everything, trail, mixing))
    solved = slab_call(everything.reshape(n_row, 1024, span), trail, inverse_factor, tokens)
    solved, weight_all = lax.optimization_barrier((solved, weight_all))
    slab_rows = lax.all_to_all(solved.reshape(n_row, 1024 // n_row, -1), "row", 0, 0)
    slab_factor = slab_rows.transpose(1, 0, 2).reshape(1024 // n_row, -1)
    pruned = jnp.concatenate(
        [lax.dynamic_slice_in_dim(weight_all, block_order[q] * NB, NB, 0) for q in range(4)], 0
    )
    own_mixing = lax.dynamic_slice_in_dim(mixing, (own % 2) * own_n, own_n, 1)
    change = lax.dot_general(own_mixing, pruned, (((0,), (0,)), ((), ())), precision=HIGH)
    return (slab_factor, (weight_t - change).T)


def solution(mesh):
    return jax.shard_map(
        on_device,
        mesh=mesh,
        in_specs=(P("row", "col"), P("row", "col"), P("row", "col"), P()),
        out_specs=(P("row", "col"), P("row", "col")),
        check_vma=False,
    )
```

```python
import functools

import jax
import jax.numpy as jnp
from jax import lax
from jax.experimental import pallas as pl
from jax.experimental.pallas import tpu as pltpu
from jax.sharding import PartitionSpec as P

f32 = jnp.float32
NB = 128
HIGH = lax.Precision.HIGHEST

def lanes(x):
    return jnp.broadcast_to(x, (8, NB))

def factor_blocks(blocks):
    lane = lax.broadcasted_iota(jnp.int32, (8, NB), 1)
    sub = lax.broadcasted_iota(jnp.int32, (8, NB), 0)
    at = [sub == k for k in range(8)]
    outs = [[] for _ in blocks]
    for j in range(16):
        lo = 8 * j
        inside = (lane >= lo) & (lane < lo + 8)
        unit = jnp.where(lane - lo == sub, 1.0, 0.0).astype(f32)
        for b, rows in enumerate(blocks):
            R = rows[j]
            D = [lanes(R[:, lo + k:lo + k + 1]) for k in range(8)]
            E = {(a, m): lanes(D[m][a:a + 1, :]) for m in range(8) for a in range(m, 8)}
            R = jnp.where(inside, unit, R)
            t = [lanes(R[k:k + 1, :]) for k in range(8)]
            inv, low = [], {}
            out = jnp.zeros((8, NB), f32)
            for k in range(8):
                p = E[k, k]
                inv.append(pl.reciprocal(p, approx=False))
                out = jnp.where(at[k], t[k] * lax.rsqrt(p), out)
                for a in range(k + 1, 8):
                    low[a, k] = E[a, k] * inv[k]
                    t[a] = t[a] - low[a, k] * t[k]
                    for m in range(k + 1, a + 1):
                        E[a, m] = E[a, m] - low[a, k] * E[m, k]
            outs[b].append(jnp.where(lane <= lo + sub, out, 0.0))
            if j < 15:
                w = [t[k] * inv[k] for k in range(8)]
                for k in range(7, 0, -1):
                    for a in range(k):
                        w[a] = w[a] - low[k, a] * w[k]
                for i in range(j + 1, 16):
                    T = rows[i]
                    terms = [lanes(T[:, lo + k:lo + k + 1]) * w[k] for k in range(7, -1, -1)]
                    T = jnp.where(inside, 0.0, T)
                    for x in terms:
                        T = T - x
                    rows[i] = T
    return outs

def load_block(ref, k):
    o = pl.multiple_of(k * NB, NB)
    return [ref[pl.ds(pl.multiple_of(o + 8 * i, 8), 8), pl.ds(o, NB)] for i in range(16)]

def split3(x):
    a = x.astype(jnp.bfloat16)
    r = x - a.astype(f32)
    b = r.astype(jnp.bfloat16)
    return a, b, (r - b.astype(f32)).astype(jnp.bfloat16)

def stack_left(x):
    a, b, c = split3(x)
    return jnp.concatenate([a, a, b, b, a, c], 1)

def stack_right(x):
    a, b, c = split3(x)
    return jnp.concatenate([a, b, a, b, c, a], 0)

def prepare(ref, inv_ref, left, right, k, n):
    o = pl.multiple_of(k * NB, NB)
    w = n * NB
    eye = jnp.where(lax.broadcasted_iota(jnp.int32, (NB, NB), 0) == lax.broadcasted_iota(jnp.int32, (NB, NB), 1), 1.0, 0.0).astype(f32)
    ref[pl.ds(o, NB), pl.ds(o, NB)] = eye
    inverse = stack_left(inv_ref[...])
    for h in range(n // 4):
        s = slice(h * 512, h * 512 + 512)
        U = jnp.dot(inverse, stack_right(ref[pl.ds(o, NB), s]), preferred_element_type=f32)
        ref[pl.ds(o, NB), s] = U
        right[:, s] = stack_right(U)
    for i in range(1, n):
        s = slice(i * NB, i * NB + NB)
        below = k < i
        left[s, :] = stack_left(jnp.where(below, ref[pl.ds(o, NB), s].T, 0.0))
        ref[s, pl.ds(o, NB)] = jnp.where(below, 0.0, ref[s, pl.ds(o, NB)])
    v = pl.multiple_of(jnp.minimum(k + 1, n - 1) * NB, NB)
    ref[pl.ds(v, NB), pl.ds(v, NB)] -= jnp.dot(left[pl.ds(v, NB), :], right[:, pl.ds(v, NB)], preferred_element_type=f32)

def update(ref, left, right, first, n):
    s = slice(first * NB, n * NB)
    ref[s, :] -= jnp.dot(left[s, :], right[...], preferred_element_type=f32)

def kernel(tokens, order_ref, own_ref, g_ref, x_out, m_ref, x_ref, at, inv1, inv2, hst, left1, right1, left2, right2, sems):
    r = lax.broadcasted_iota(jnp.int32, (NB, NB), 0)
    c = lax.broadcasted_iota(jnp.int32, (NB, NB), 1)
    diag = r == c
    tot = jnp.zeros((NB, NB), f32)
    for b in range(8):
        tot += jnp.where(diag, g_ref[b * NB:(b + 1) * NB, :NB], 0.0)
    scale = 1.0 / tokens
    damp = jnp.sum(tot) * (0.01 / 1024.0 / tokens)
    for a in range(8):
        for b in range(a, 8):
            if b - a <= 4:
                v = g_ref[a * NB:(a + 1) * NB, (b - a) * NB:(b - a + 1) * NB]
            else:
                v = g_ref[b * NB:(b + 1) * NB, (8 + a - b) * NB:(9 + a - b) * NB].T
            v = v * scale
            if a == b:
                v = v + jnp.where(diag, damp, 0.0)
            x_ref[a * NB:(a + 1) * NB, b * NB:(b + 1) * NB] = v
    for a in range(4):
        ta, sa = order_ref[4 + a], order_ref[a]
        oa = pl.multiple_of(ta * NB, NB)
        os = pl.multiple_of(sa * NB, NB)
        for b in range(4):
            tb = order_ref[4 + b]
            ob = pl.multiple_of(tb * NB, NB)
            if a <= b:
                at[a * NB:(a + 1) * NB, b * NB:(b + 1) * NB] = x_ref[pl.ds(oa, NB), pl.ds(ob, NB)]

            @pl.when(sa < tb)
            def _():
                hst[a * NB:(a + 1) * NB, b * NB:(b + 1) * NB] = x_ref[pl.ds(os, NB), pl.ds(ob, NB)]

            @pl.when(sa > tb)
            def _():
                hst[a * NB:(a + 1) * NB, b * NB:(b + 1) * NB] = x_ref[pl.ds(ob, NB), pl.ds(os, NB)].T

    left1[...] = jnp.zeros_like(left1)
    right1[...] = jnp.zeros_like(right1)
    left2[...] = jnp.zeros_like(left2)
    right2[...] = jnp.zeros_like(right2)

    def send(k):
        o = pl.multiple_of(k * NB, NB)
        return pltpu.make_async_copy(x_ref.at[pl.ds(o, NB), :], x_out.at[pl.ds(o, NB), :], sems.at[k])

    def finish(k):
        o = pl.multiple_of(k * NB, NB)

        @pl.when(lax.rem(k, 2) == 0)
        def _():
            x_ref[pl.ds(o, NB), pl.ds(pl.multiple_of(o + NB, NB), NB)] = jnp.zeros((NB, NB), f32)
        send(k).start()

    def both(k, _):
        b1, b2 = load_block(x_ref, k), load_block(at, k)
        update(x_ref, left1, right1, 1, 8)
        update(at, left2, right2, 1, 4)
        o1, o2 = factor_blocks([b1, b2])
        for i in range(16):
            inv1[8 * i:8 * i + 8, :] = o1[i]
            inv2[8 * i:8 * i + 8, :] = o2[i]
        prepare(x_ref, inv1, left1, right1, k, 8)
        prepare(at, inv2, left2, right2, k, 4)
        finish(k)
        return 0
    lax.fori_loop(0, 4, both, 0)

    def single(k, _):
        b1 = load_block(x_ref, k)
        update(x_ref, left1, right1, 4, 8)
        o1, = factor_blocks([b1])
        for i in range(16):
            inv1[8 * i:8 * i + 8, :] = o1[i]
        prepare(x_ref, inv1, left1, right1, k, 8)
        finish(k)
        return 0
    lax.fori_loop(4, 8, single, 0)
    for k in range(3):
        at[k * NB:(k + 1) * NB, (k + 1) * NB:] = jnp.zeros((NB, (3 - k) * NB), f32)
    own = own_ref[0]
    for a in range(4):
        @pl.when(order_ref[a] == own)
        def _():
            m_ref[...] = jnp.zeros((512, NB), f32)
            m_ref[a * NB:(a + 1) * NB, :] = jnp.where(diag, 1.0, 0.0)
        @pl.when(order_ref[4 + a] == own)
        def _():
            z = lax.dot_general(at[...], at[:, a * NB:(a + 1) * NB], (((0,), (0,)), ((), ())), precision=HIGH, preferred_element_type=f32)
            m_ref[...] = -jnp.dot(hst[...], z, precision=HIGH, preferred_element_type=f32)
    for k in range(8):
        send(k).wait()

def factor_call(gram, order, own, tokens):
    bf16 = jnp.bfloat16
    return pl.pallas_call(
        functools.partial(kernel, tokens),
        out_shape=(jax.ShapeDtypeStruct((1024, 1024), f32), jax.ShapeDtypeStruct((512, NB), f32)),
        in_specs=[pl.BlockSpec(memory_space=pltpu.SMEM), pl.BlockSpec(memory_space=pltpu.SMEM), pl.BlockSpec(memory_space=pltpu.VMEM)],
        out_specs=(pl.BlockSpec(memory_space=pltpu.MemorySpace.HBM), pl.BlockSpec(memory_space=pltpu.VMEM)),
        scratch_shapes=[
            pltpu.VMEM((1024, 1024), f32), pltpu.VMEM((512, 512), f32), pltpu.VMEM((NB, NB), f32), pltpu.VMEM((NB, NB), f32),
            pltpu.VMEM((512, 512), f32), pltpu.VMEM((1024, 768), bf16), pltpu.VMEM((768, 1024), bf16),
            pltpu.VMEM((512, 768), bf16), pltpu.VMEM((768, 512), bf16), pltpu.SemaphoreType.DMA((8,)),
        ],
        compiler_params=pltpu.CompilerParams(vmem_limit_bytes=40 * 1024 * 1024),
    )(order, own, gram)


def slab_kernel(tokens, panel_ref, trail_ref, inverse_ref, out_ref, total, inverse, sem):
    copy = pltpu.make_async_copy(inverse_ref, inverse, sem)

    @pl.when(pl.program_id(0) == 0)
    def _():
        copy.start()
        total[...] = jnp.zeros_like(total)

    part = jnp.dot(panel_ref[0], trail_ref[0], preferred_element_type=f32)
    for g in range(1, panel_ref.shape[0]):
        part += jnp.dot(panel_ref[g], trail_ref[g], preferred_element_type=f32)
    total[...] += part

    @pl.when(pl.program_id(0) == pl.num_programs(0) - 1)
    def _():
        copy.wait()
        slab = total[...] * (1.0 / tokens)
        for h in range(4):
            s = slice(256 * h, 256 * h + 256)
            e = 256 * h + 256
            out_ref[s, :] = jnp.dot(inverse[s, :e], slab[:e], precision=HIGH, preferred_element_type=f32)


def slab_call(panel, trail, inverse, tokens):
    groups, channels, span = panel.shape
    columns = trail.shape[2]
    each = 2
    return pl.pallas_call(
        functools.partial(slab_kernel, tokens),
        grid=(groups // each,),
        in_specs=[
            pl.BlockSpec((each, channels, span), lambda i: (i, 0, 0)),
            pl.BlockSpec((each, span, columns), lambda i: (i, 0, 0)),
            pl.BlockSpec(memory_space=pltpu.MemorySpace.HBM),
        ],
        out_specs=pl.BlockSpec((channels, columns), lambda i: (0, 0)),
        out_shape=jax.ShapeDtypeStruct((channels, columns), f32),
        scratch_shapes=[
            pltpu.VMEM((channels, columns), f32),
            pltpu.VMEM((channels, channels), f32),
            pltpu.SemaphoreType.DMA,
        ],
        compiler_params=pltpu.CompilerParams(vmem_limit_bytes=40 * 1024 * 1024),
    )(panel, trail, inverse)


def spread(x, axis):
    n = lax.axis_size(axis)
    return lax.all_to_all(jnp.broadcast_to(x[None], (n,) + x.shape), axis, 0, 0)


def ascending(blocks):
    place = jnp.sum((blocks[None, :] < blocks[:, None]).astype(jnp.int32), 1)
    slot = jnp.arange(blocks.shape[0], dtype=jnp.int32)
    return jnp.sum(jnp.where(place[None, :] == slot[:, None], blocks[None, :], 0), 1)


def on_device(acts_panel, acts_trail, weight_panel, block_order):
    n_row = lax.axis_size("row")
    span, own_n = acts_panel.shape
    tokens = span * n_row
    own = lax.axis_index("col")
    own_t = acts_panel.T
    everything = lax.all_gather(own_t, ("row", "col"))
    panel_t = spread(own_t, "col").reshape(-1, span)
    strip = lax.dot_general(own_t, panel_t, (((1,), (1,)), ((), ())), preferred_element_type=f32)
    pieces = strip.reshape(8, 8, 2, 512).transpose(0, 2, 1, 3).reshape(16, 8, 512)
    piece = lax.all_to_all(pieces, "row", 0, 0).sum(0)
    strip_total = spread(piece, "row").reshape(8, 2, 8, 512).transpose(0, 2, 1, 3).reshape(64, 1024)
    twice = jnp.concatenate([strip_total, strip_total[:, :512]], 1)
    band = lax.dynamic_slice_in_dim(twice, own // 2 * NB, 5 * NB, 1)
    gram = spread(band, "col").reshape(1024, 5 * NB)
    weight_t = weight_panel.T
    columns = acts_trail.shape[1] // n_row
    trail_cut = acts_trail.reshape(span, n_row, columns).transpose(1, 0, 2)
    weight_in, trail_cut, gram = lax.optimization_barrier((weight_t, trail_cut, gram))
    trail = lax.all_to_all(trail_cut, "row", 0, 0)
    weight_all = lax.all_gather(weight_in, "col", axis=0, tiled=True)
    order = jnp.concatenate([block_order[:4], ascending(block_order[4:])])
    inverse_factor, mixing = factor_call(gram, order, (own // 2).reshape(1), tokens)
    everything, trail, mixing = lax.optimization_barrier((everything, trail, mixing))
    solved = slab_call(everything.reshape(n_row, 1024, span), trail, inverse_factor, tokens)
    slab_rows = lax.all_to_all(solved.reshape(n_row, 1024 // n_row, -1), "row", 0, 0)
    slab_factor = slab_rows.transpose(1, 0, 2).reshape(1024 // n_row, -1)
    pruned = jnp.concatenate(
        [lax.dynamic_slice_in_dim(weight_all, block_order[q] * NB, NB, 0) for q in range(4)], 0
    )
    own_mixing = lax.dynamic_slice_in_dim(mixing, (own % 2) * own_n, own_n, 1)
    change = lax.dot_general(own_mixing, pruned, (((0,), (0,)), ((), ())), precision=HIGH)
    return (slab_factor, (weight_t - change).T)


def solution(mesh):
    return jax.shard_map(
        on_device,
        mesh=mesh,
        in_specs=(P("row", "col"), P("row", "col"), P("row", "col"), P()),
        out_specs=(P("row", "col"), P("row", "col")),
        check_vma=False,
    )
```

```python
import functools

import jax
import jax.numpy as jnp
from jax import lax
from jax.experimental import pallas as pl
from jax.experimental.pallas import tpu as pltpu
from jax.sharding import PartitionSpec as P

f32 = jnp.float32
NB = 128
HIGH = lax.Precision.HIGHEST

def lanes(x):
    return jnp.broadcast_to(x, (8, NB))

def factor_blocks(blocks):
    lane = lax.broadcasted_iota(jnp.int32, (8, NB), 1)
    sub = lax.broadcasted_iota(jnp.int32, (8, NB), 0)
    at = [sub == k for k in range(8)]
    outs = [[] for _ in blocks]
    for j in range(16):
        lo = 8 * j
        inside = (lane >= lo) & (lane < lo + 8)
        unit = jnp.where(lane - lo == sub, 1.0, 0.0).astype(f32)
        for b, rows in enumerate(blocks):
            R = rows[j]
            D = [lanes(R[:, lo + k:lo + k + 1]) for k in range(8)]
            E = {(a, m): lanes(D[m][a:a + 1, :]) for m in range(8) for a in range(m, 8)}
            R = jnp.where(inside, unit, R)
            t = [lanes(R[k:k + 1, :]) for k in range(8)]
            inv, low = [], {}
            out = jnp.zeros((8, NB), f32)
            for k in range(8):
                p = E[k, k]
                inv.append(pl.reciprocal(p, approx=False))
                out = jnp.where(at[k], t[k] * lax.rsqrt(p), out)
                for a in range(k + 1, 8):
                    low[a, k] = E[a, k] * inv[k]
                    t[a] = t[a] - low[a, k] * t[k]
                    for m in range(k + 1, a + 1):
                        E[a, m] = E[a, m] - low[a, k] * E[m, k]
            outs[b].append(jnp.where(lane <= lo + sub, out, 0.0))
            if j < 15:
                w = [t[k] * inv[k] for k in range(8)]
                for k in range(7, 0, -1):
                    for a in range(k):
                        w[a] = w[a] - low[k, a] * w[k]
                for i in range(j + 1, 16):
                    T = rows[i]
                    terms = [lanes(T[:, lo + k:lo + k + 1]) * w[k] for k in range(7, -1, -1)]
                    T = jnp.where(inside, 0.0, T)
                    for x in terms:
                        T = T - x
                    rows[i] = T
    return outs

def load_block(ref, k):
    o = pl.multiple_of(k * NB, NB)
    return [ref[pl.ds(pl.multiple_of(o + 8 * i, 8), 8), pl.ds(o, NB)] for i in range(16)]

def split3(x):
    a = x.astype(jnp.bfloat16)
    r = x - a.astype(f32)
    b = r.astype(jnp.bfloat16)
    return a, b, (r - b.astype(f32)).astype(jnp.bfloat16)

def stack_left(x):
    a, b, c = split3(x)
    return jnp.concatenate([a, a, b, b, a, c], 1)

def stack_right(x):
    a, b, c = split3(x)
    return jnp.concatenate([a, b, a, b, c, a], 0)

def prepare(ref, inv_ref, left, right, k, n):
    o = pl.multiple_of(k * NB, NB)
    w = n * NB
    eye = jnp.where(lax.broadcasted_iota(jnp.int32, (NB, NB), 0) == lax.broadcasted_iota(jnp.int32, (NB, NB), 1), 1.0, 0.0).astype(f32)
    ref[pl.ds(o, NB), pl.ds(o, NB)] = eye
    inverse = stack_left(inv_ref[...])
    for h in range(n // 4):
        s = slice(h * 512, h * 512 + 512)
        U = jnp.dot(inverse, stack_right(ref[pl.ds(o, NB), s]), preferred_element_type=f32)
        ref[pl.ds(o, NB), s] = U
        right[:, s] = stack_right(U)
    for i in range(1, n):
        s = slice(i * NB, i * NB + NB)
        below = k < i
        left[s, :] = stack_left(jnp.where(below, ref[pl.ds(o, NB), s].T, 0.0))
        ref[s, pl.ds(o, NB)] = jnp.where(below, 0.0, ref[s, pl.ds(o, NB)])
    v = pl.multiple_of(jnp.minimum(k + 1, n - 1) * NB, NB)
    ref[pl.ds(v, NB), pl.ds(v, NB)] -= jnp.dot(left[pl.ds(v, NB), :], right[:, pl.ds(v, NB)], preferred_element_type=f32)

def update(ref, left, right, first, n):
    s = slice(first * NB, n * NB)
    ref[s, :] -= jnp.dot(left[s, :], right[...], preferred_element_type=f32)

def kernel(tokens, order_ref, own_ref, g_ref, x_out, m_ref, x_ref, at, inv1, inv2, hst, left1, right1, left2, right2, sems):
    r = lax.broadcasted_iota(jnp.int32, (NB, NB), 0)
    c = lax.broadcasted_iota(jnp.int32, (NB, NB), 1)
    diag = r == c
    tot = jnp.zeros((NB, NB), f32)
    for b in range(8):
        tot += jnp.where(diag, g_ref[b * NB:(b + 1) * NB, :NB], 0.0)
    scale = 1.0 / tokens
    damp = jnp.sum(tot) * (0.01 / 1024.0 / tokens)
    for a in range(8):
        for b in range(a, 8):
            if b - a <= 4:
                v = g_ref[a * NB:(a + 1) * NB, (b - a) * NB:(b - a + 1) * NB]
            else:
                v = g_ref[b * NB:(b + 1) * NB, (8 + a - b) * NB:(9 + a - b) * NB].T
            v = v * scale
            if a == b:
                v = v + jnp.where(diag, damp, 0.0)
            x_ref[a * NB:(a + 1) * NB, b * NB:(b + 1) * NB] = v
    for a in range(4):
        ta, sa = order_ref[4 + a], order_ref[a]
        oa = pl.multiple_of(ta * NB, NB)
        os = pl.multiple_of(sa * NB, NB)
        for b in range(4):
            tb = order_ref[4 + b]
            ob = pl.multiple_of(tb * NB, NB)
            if a <= b:
                at[a * NB:(a + 1) * NB, b * NB:(b + 1) * NB] = x_ref[pl.ds(oa, NB), pl.ds(ob, NB)]

            @pl.when(sa < tb)
            def _():
                hst[a * NB:(a + 1) * NB, b * NB:(b + 1) * NB] = x_ref[pl.ds(os, NB), pl.ds(ob, NB)]

            @pl.when(sa > tb)
            def _():
                hst[a * NB:(a + 1) * NB, b * NB:(b + 1) * NB] = x_ref[pl.ds(ob, NB), pl.ds(os, NB)].T

    left1[...] = jnp.zeros_like(left1)
    right1[...] = jnp.zeros_like(right1)
    left2[...] = jnp.zeros_like(left2)
    right2[...] = jnp.zeros_like(right2)

    def send(k):
        o = pl.multiple_of(k * NB, NB)
        return pltpu.make_async_copy(x_ref.at[pl.ds(o, NB), :], x_out.at[pl.ds(o, NB), :], sems.at[k])

    def finish(k):
        o = pl.multiple_of(k * NB, NB)

        @pl.when(lax.rem(k, 2) == 0)
        def _():
            x_ref[pl.ds(o, NB), pl.ds(pl.multiple_of(o + NB, NB), NB)] = jnp.zeros((NB, NB), f32)
        send(k).start()

    def both(k, _):
        b1, b2 = load_block(x_ref, k), load_block(at, k)
        update(x_ref, left1, right1, 1, 8)
        update(at, left2, right2, 1, 4)
        o1, o2 = factor_blocks([b1, b2])
        for i in range(16):
            inv1[8 * i:8 * i + 8, :] = o1[i]
            inv2[8 * i:8 * i + 8, :] = o2[i]
        prepare(x_ref, inv1, left1, right1, k, 8)
        prepare(at, inv2, left2, right2, k, 4)
        finish(k)
        return 0
    lax.fori_loop(0, 4, both, 0)

    def single(k, _):
        b1 = load_block(x_ref, k)
        update(x_ref, left1, right1, 4, 8)
        o1, = factor_blocks([b1])
        for i in range(16):
            inv1[8 * i:8 * i + 8, :] = o1[i]
        prepare(x_ref, inv1, left1, right1, k, 8)
        finish(k)
        return 0
    lax.fori_loop(4, 8, single, 0)
    for k in range(3):
        at[k * NB:(k + 1) * NB, (k + 1) * NB:] = jnp.zeros((NB, (3 - k) * NB), f32)
    own = own_ref[0]
    for a in range(4):
        @pl.when(order_ref[a] == own)
        def _():
            m_ref[...] = jnp.zeros((512, NB), f32)
            m_ref[a * NB:(a + 1) * NB, :] = jnp.where(diag, 1.0, 0.0)
        @pl.when(order_ref[4 + a] == own)
        def _():
            z = lax.dot_general(at[...], at[:, a * NB:(a + 1) * NB], (((0,), (0,)), ((), ())), precision=HIGH, preferred_element_type=f32)
            m_ref[...] = -jnp.dot(hst[...], z, precision=HIGH, preferred_element_type=f32)
    for k in range(8):
        send(k).wait()

def factor_call(gram, order, own, tokens):
    bf16 = jnp.bfloat16
    return pl.pallas_call(
        functools.partial(kernel, tokens),
        out_shape=(jax.ShapeDtypeStruct((1024, 1024), f32), jax.ShapeDtypeStruct((512, NB), f32)),
        in_specs=[pl.BlockSpec(memory_space=pltpu.SMEM), pl.BlockSpec(memory_space=pltpu.SMEM), pl.BlockSpec(memory_space=pltpu.VMEM)],
        out_specs=(pl.BlockSpec(memory_space=pltpu.MemorySpace.HBM), pl.BlockSpec(memory_space=pltpu.VMEM)),
        scratch_shapes=[
            pltpu.VMEM((1024, 1024), f32), pltpu.VMEM((512, 512), f32), pltpu.VMEM((NB, NB), f32), pltpu.VMEM((NB, NB), f32),
            pltpu.VMEM((512, 512), f32), pltpu.VMEM((1024, 768), bf16), pltpu.VMEM((768, 1024), bf16),
            pltpu.VMEM((512, 768), bf16), pltpu.VMEM((768, 512), bf16), pltpu.SemaphoreType.DMA((8,)),
        ],
        compiler_params=pltpu.CompilerParams(vmem_limit_bytes=40 * 1024 * 1024),
    )(order, own, gram)


def slab_kernel(tokens, panel_ref, trail_ref, inverse_ref, out_ref, total, inverse, sem):
    copy = pltpu.make_async_copy(inverse_ref, inverse, sem)

    @pl.when(pl.program_id(0) == 0)
    def _():
        copy.start()
        total[...] = jnp.zeros_like(total)

    part = jnp.dot(panel_ref[0], trail_ref[0], preferred_element_type=f32)
    for g in range(1, panel_ref.shape[0]):
        part += jnp.dot(panel_ref[g], trail_ref[g], preferred_element_type=f32)
    total[...] += part

    @pl.when(pl.program_id(0) == pl.num_programs(0) - 1)
    def _():
        copy.wait()
        slab = total[...] * (1.0 / tokens)
        for h in range(4):
            s = slice(256 * h, 256 * h + 256)
            e = 256 * h + 256
            out_ref[s, :] = jnp.dot(inverse[s, :e], slab[:e], precision=HIGH, preferred_element_type=f32)


def slab_call(panel, trail, inverse, tokens):
    groups, channels, span = panel.shape
    columns = trail.shape[2]
    each = 2
    return pl.pallas_call(
        functools.partial(slab_kernel, tokens),
        grid=(groups // each,),
        in_specs=[
            pl.BlockSpec((each, channels, span), lambda i: (i, 0, 0)),
            pl.BlockSpec((each, span, columns), lambda i: (i, 0, 0)),
            pl.BlockSpec(memory_space=pltpu.MemorySpace.HBM),
        ],
        out_specs=pl.BlockSpec((channels, columns), lambda i: (0, 0)),
        out_shape=jax.ShapeDtypeStruct((channels, columns), f32),
        scratch_shapes=[
            pltpu.VMEM((channels, columns), f32),
            pltpu.VMEM((channels, channels), f32),
            pltpu.SemaphoreType.DMA,
        ],
        compiler_params=pltpu.CompilerParams(vmem_limit_bytes=40 * 1024 * 1024),
    )(panel, trail, inverse)


def spread(x, axis):
    n = lax.axis_size(axis)
    return lax.all_to_all(jnp.broadcast_to(x[None], (n,) + x.shape), axis, 0, 0)


def ascending(blocks):
    place = jnp.sum((blocks[None, :] < blocks[:, None]).astype(jnp.int32), 1)
    slot = jnp.arange(blocks.shape[0], dtype=jnp.int32)
    return jnp.sum(jnp.where(place[None, :] == slot[:, None], blocks[None, :], 0), 1)


def on_device(acts_panel, acts_trail, weight_panel, block_order):
    n_row = lax.axis_size("row")
    span, own_n = acts_panel.shape
    tokens = span * n_row
    own = lax.axis_index("col")
    own_t = acts_panel.T
    everything = lax.all_gather(own_t, ("row", "col"))
    panel_t = spread(own_t, "col").reshape(-1, span)
    strip = lax.dot_general(own_t, panel_t, (((1,), (1,)), ((), ())), preferred_element_type=f32)
    pieces = strip.reshape(8, 8, 2, 512).transpose(0, 2, 1, 3).reshape(16, 8, 512)
    piece = lax.all_to_all(pieces, "row", 0, 0).sum(0)
    strip_total = spread(piece, "row").reshape(8, 2, 8, 512).transpose(0, 2, 1, 3).reshape(64, 1024)
    twice = jnp.concatenate([strip_total, strip_total[:, :512]], 1)
    band = lax.dynamic_slice_in_dim(twice, own // 2 * NB, 5 * NB, 1)
    gram = spread(band, "col").reshape(1024, 5 * NB)
    weight_t = weight_panel.T
    columns = acts_trail.shape[1] // n_row
    trail_cut = acts_trail.reshape(span, n_row, columns).transpose(1, 0, 2)
    weight_in, trail_cut, gram = lax.optimization_barrier((weight_t, trail_cut, gram))
    trail = lax.all_to_all(trail_cut, "row", 0, 0)
    weight_all = lax.all_gather(weight_in, "col", axis=0, tiled=True)
    order = jnp.concatenate([block_order[:4], ascending(block_order[4:])])
    inverse_factor, mixing = factor_call(gram, order, (own // 2).reshape(1), tokens)
    everything, trail, mixing = lax.optimization_barrier((everything, trail, mixing))
    solved = slab_call(everything.reshape(n_row, 1024, span), trail, inverse_factor, tokens)
    slab_rows = lax.all_to_all(solved.reshape(n_row, 1024 // n_row, -1), "row", 0, 0)
    slab_factor = slab_rows.transpose(1, 0, 2).reshape(1024 // n_row, -1)
    slab_factor, weight_all = lax.optimization_barrier((slab_factor, weight_all))
    pruned = jnp.concatenate(
        [lax.dynamic_slice_in_dim(weight_all, block_order[q] * NB, NB, 0) for q in range(4)], 0
    )
    own_mixing = lax.dynamic_slice_in_dim(mixing, (own % 2) * own_n, own_n, 1)
    change = lax.dot_general(own_mixing, pruned, (((0,), (0,)), ((), ())), precision=HIGH)
    return (slab_factor, (weight_t - change).T)


def solution(mesh):
    return jax.shard_map(
        on_device,
        mesh=mesh,
        in_specs=(P("row", "col"), P("row", "col"), P("row", "col"), P()),
        out_specs=(P("row", "col"), P("row", "col")),
        check_vma=False,
    )
```
